256 devices in a mesh: gx: 8 (over x, z_hi), gy: 8 (over y, core), gz: 4 (over z_lo).
Axes of the slice: x: 4, y: 4, z: 8 (z_hi: 2, z_lo: 4; z = z_hi * 4 + z_lo), core: 2. Of those that a mesh axis runs over, the one named last changes fastest.
Arguments:
- tokens: bfloat16 [1536, 4096], P(('gx', 'gy'), 'gz'), may hold values from -6 to 6
- gate_weight: bfloat16 [4096, 16384], P('gz', ('gx', 'gy')), may hold values from -0.09375 to 0.09375
- up_weight: bfloat16 [4096, 16384], P('gz', ('gx', 'gy')), may hold values from -0.09375 to 0.09375
- down_weight: bfloat16 [4096, 16384], P('gz', ('gx', 'gy')), may hold values from -0.046875 to 0.046875
- grad_out: bfloat16 [1536, 4096], P(('gx', 'gy'), 'gz'), may hold values from -6 to 6
Outputs:
- block_out: bfloat16 [1536, 4096], P(('gx', 'gy'), 'gz')
- grad_tokens: bfloat16 [1536, 4096], P(('gx', 'gy'), 'gz')
- grad_gate: float32 [4096, 16384], P('gz', ('gx', 'gy'))
- grad_up: float32 [4096, 16384], P('gz', ('gx', 'gy'))
- grad_down: float32 [4096, 16384], P('gz', ('gx', 'gy'))
The draws below stay inside these ranges and needn't reach their ends.
All inputs are finite; a program needn't handle non-finite values.
Results may differ from the reference program's by a relative error of at most 0.013.
Values may be sent and summed in bfloat16 or wider, within the bound.
A program may use at most 128 MiB of HBM per device.

```python
import jax
import jax.numpy as jnp
from jax import lax

D = 4096
FF = 16384
TOKENS = 1536


def block_scale(own_key, shape, cuts, smallest, largest):
    factor_of = 1.0
    for position, blocks in cuts:
        heights = jax.random.uniform(jax.random.fold_in(jax.random.fold_in(own_key, 6), position), (blocks,), jnp.float32, smallest / len(cuts), largest / len(cuts))
        factor_of = factor_of * jnp.repeat(jnp.exp(heights), shape[position] // blocks).reshape((-1,) + (1,) * (len(shape) - 1 - position))
    return factor_of


def bell_draw(key, dims, width, limit, split=(), held_as=jnp.bfloat16):
    loudness = block_scale(key, dims, split, -0.22, 0.18) if split else 1.0
    array = jax.random.normal(key, dims, jnp.float32) * width * loudness
    return jnp.minimum(jnp.maximum(array, -limit), limit).astype(held_as)


def setup_inputs(seed: int = 0) -> dict:
    key_list = jax.random.split(jax.random.key(seed), 6)
    tokens = bell_draw(key_list[0], (TOKENS, D), 1.0, 6.0, ((0, 64), (1, 4)))
    gate_weight = bell_draw(key_list[1], (D, FF), D ** -0.5, 0.09375, ((0, 4), (1, 64)))
    up_weight = bell_draw(key_list[2], (D, FF), D ** -0.5, 0.09375, ((0, 4), (1, 64)))
    down_weight = bell_draw(key_list[3], (D, FF), FF ** -0.5, 0.046875, ((0, 4), (1, 64)))
    grad_out = bell_draw(key_list[4], (TOKENS, D), 1.0, 6.0, ((0, 64), (1, 4)))
    return dict(tokens=tokens, gate_weight=gate_weight, up_weight=up_weight, down_weight=down_weight, grad_out=grad_out)


def rows_by_rows(left, right):
    return lax.dot_general(left, right, (((1,), (1,)), ((), ())), preferred_element_type=jnp.float32)


def cols_by_cols(left, right):
    return lax.dot_general(left, right, (((0,), (0,)), ((), ())), preferred_element_type=jnp.float32)


def reference(tokens, gate_weight, up_weight, down_weight, grad_out):
    gate_sum = jnp.dot(tokens, gate_weight, preferred_element_type=jnp.float32)
    up_sum = jnp.dot(tokens, up_weight, preferred_element_type=jnp.float32)
    sigmoid_gate = 1.0 / (1.0 + jnp.exp(-gate_sum))
    silu_gate = gate_sum * sigmoid_gate
    hidden = (silu_gate * up_sum).astype(jnp.bfloat16)
    projected = rows_by_rows(hidden, down_weight)
    block_out = (tokens.astype(jnp.float32) + projected).astype(jnp.bfloat16)
    hidden_grad = jnp.dot(grad_out, down_weight, preferred_element_type=jnp.float32)
    gate_grad = (hidden_grad * up_sum * sigmoid_gate * (1.0 + gate_sum * (1.0 - sigmoid_gate))).astype(jnp.bfloat16)
    up_part_grad = (hidden_grad * silu_gate).astype(jnp.bfloat16)
    backward = rows_by_rows(gate_grad, gate_weight) + rows_by_rows(up_part_grad, up_weight)
    grad_tokens = (grad_out.astype(jnp.float32) + backward).astype(jnp.bfloat16)
    grad_gate = cols_by_cols(tokens, gate_grad)
    grad_up = cols_by_cols(tokens, up_part_grad)
    grad_down = cols_by_cols(grad_out, hidden)
    return block_out, grad_tokens, grad_gate, grad_up, grad_down
```

```python
import functools

import jax
import jax.numpy as jnp
from jax import lax
from jax.experimental import pallas as pl
from jax.experimental.pallas import tpu as pltpu
from jax.sharding import PartitionSpec as P

MESH = pl.DeviceIdType.MESH
F32 = jnp.float32
BF16 = jnp.bfloat16
CHUNKS = 8


def chunk_place(k):
    pair, odd = k // 2, k % 2
    first = 1 - (pair + 2) // 3
    last = pair // 3
    third = pair // 2 - last
    dzh = first * odd + third + last * (1 - odd)
    dy = (1 - first - last) * (1 + 2 * odd) + 2 * last
    return dzh, dy


def dot_nn(a, b):
    return jnp.dot(a, b, preferred_element_type=F32)


def dot_nt(a, b):
    return lax.dot_general(a, b, (((1,), (1,)), ((), ())), preferred_element_type=F32)


def dot_tn(a, b):
    return lax.dot_general(a, b, (((0,), (0,)), ((), ())), preferred_element_type=F32)


def body(
    tok, grd, wg_any, wu_any, wd_any,
    out, gtok, d_gate, d_up, d_down,
    wg, wu, wd, mine, theirs, gath, part, zsend, zin1, zin2, res,
    both, cin, xsend, xin, ysend, yin, zhs, zhin, fin, fin_in,
    w_sem, cx, zx, xa, ya, fw, z1, z2, z3, co, xr, yr, zr, fo,
):
    gx, gy, zl = lax.axis_index("gx"), lax.axis_index("gy"), lax.axis_index("gz")
    x, zh, y, c = gx // 2, gx % 2, gy // 2, gy % 2
    units = wg.shape[1]
    feats = wg.shape[0]
    rows = gath.shape[2] * gath.shape[3]

    def at(x_, zh_, y_, c_, zl_):
        return (x_ * 2 + zh_, y_ * 2 + c_, zl_)

    def x_peer(j):
        return at((x + j) % 4, zh, y, c, zl)

    def y_peer(j):
        return at(x, zh, (y + j) % 4, c, zl)

    core_peer = at(x, zh, y, 1 - c, zl)
    half_peer = at(x, 1 - zh, y, c, zl)
    pair_z = zl + 1 - 2 * (zl % 2)
    pair_peer = at(x, zh, y, c, pair_z)
    mid_peer = at(x, zh, y, c, 3 - zl)
    is_mid = ((zl + 1) // 2) % 2 == 1
    is_end = ((zl + 1) // 2) % 2 == 0

    def send(src, dst, sems, idx, peer):
        return pltpu.make_async_remote_copy(
            src_ref=src, dst_ref=dst, send_sem=sems.at[(0, *idx)], recv_sem=sems.at[(1, *idx)],
            device_id=peer, device_id_type=MESH,
        )

    def slot(k):
        dzh, dy = chunk_place(k)
        return ((zh + dzh) % 2) * 4 + (y + dy) % 4

    def core_copy():
        return send(mine, theirs, cx, (0,), core_peer)

    def half_copy(place):
        return send(gath.at[c, place, x], gath.at[c, place, x], zx, (0,), half_peer)

    def gather_x(dzh, j, owner):
        place = ((zh + dzh) % 2) * 4 + y
        return send(gath.at[c, place, owner], gath.at[c, place, owner], xa, (dzh, j - 1), x_peer(-j))

    def gather_y(k, place, dy):
        return send(gath.at[c, place], gath.at[c, place], ya, (k,), y_peer(4 - dy))

    def forward(k, which):
        return send(gath.at[which, slot(k)], gath.at[which, slot(k)], fw, (k,), core_peer)

    def to_pair(k):
        return send(zsend.at[k], zin1.at[k], z1, (k,), pair_peer)

    def to_mid(k):
        return send(zsend.at[k], zin2.at[k], z2, (k,), mid_peer)

    def to_end(k):
        return send(res.at[k], res.at[k], z3, (k,), pair_peer)

    def to_core(k):
        return send(both.at[k, 1 - c], cin.at[k], co, (k,), core_peer)

    def scatter_x(k, j):
        return send(xsend.at[k, (x + j) % 4], xin.at[k, j - 1], xr, (k, j - 1), x_peer(j))

    def scatter_y(k):
        _, dy = chunk_place(k)
        return send(ysend.at[k], yin.at[k], yr, (k,), y_peer(dy))

    def half_back():
        return send(zhs, zhin, zr, (0,), half_peer)

    def last_copy():
        return send(fin, fin_in, fo, (0,), core_peer)

    weight_copies = [
        pltpu.make_async_copy(src, dst, w_sem.at[n])
        for n, (src, dst) in enumerate(((wg_any, wg), (wu_any, wu), (wd_any, wd)))
    ]
    for cp in weight_copies:
        cp.start()

    peers = [core_peer, half_peer, pair_peer, mid_peer]
    peers += [x_peer(j) for j in (1, 2, 3)] + [y_peer(j) for j in (1, 2, 3)]
    barrier = pltpu.get_barrier_semaphore()
    for peer in peers:
        pl.semaphore_signal(barrier, inc=1, device_id=peer, device_id_type=MESH)
    mine[...] = jnp.concatenate([tok[...].astype(F32), grd[...].astype(F32)], axis=0).astype(BF16)
    pl.semaphore_wait(barrier, len(peers))

    core_copy().start()
    core_copy().wait_recv()
    m, t = mine[...].astype(F32), theirs[...].astype(F32)
    half = m.shape[0] // 2
    lo = jnp.where(c == 0, m[:half], t[half:])
    hi = jnp.where(c == 0, t[:half], m[half:])
    own = zh * 4 + y
    other = (1 - zh) * 4 + y
    gath[c, own, x] = jnp.concatenate([lo, hi], axis=0).astype(BF16)
    half_copy(own).start()
    for j in (1, 3, 2):
        gather_x(0, j, x).start()
    d_gate[...] = jnp.zeros_like(d_gate)
    d_up[...] = jnp.zeros_like(d_up)
    d_down[...] = jnp.zeros_like(d_down)
    for cp in weight_copies:
        cp.wait()
    for j in (1, 3, 2):
        gather_x(0, j, (x + j) % 4).wait_recv()
    forward(0, c).start()

    def gather_send(k):
        dzh, dy = chunk_place(k)
        gather_y(k, ((zh + dzh) % 2) * 4 + y, dy).start()

    gather_send(2)
    gather_send(3)

    def stage_partial(k):
        forward(k, 1 - c).wait_recv()
        s = slot(k)
        xs = gath[0, s].reshape(rows, feats)
        ys = gath[1, s].reshape(rows, feats)
        for n, (a, w) in enumerate(((xs, wg), (xs, wu), (ys, wd))):
            p = dot_nn(a, w[...])
            part[k, n] = p
            zsend[k, n] = p.astype(BF16)

        @pl.when(is_end)
        def _():
            to_pair(k).start()

    def stage_forward(k):
        @pl.when(k == 1)
        def _():
            half_copy(other).wait_recv()
            for j in (1, 3, 2):
                gather_x(1, j, x).start()
            for j in (1, 3, 2):
                gather_x(1, j, (x + j) % 4).wait_recv()

        @pl.when(k >= 2)
        def _():
            gather_y(k, slot(k), 0).wait_recv()

        forward(k, c).start()

    def stage_pair(k):
        to_pair(k).wait_recv()
        for n in range(3):
            a = part[k, n] + zin1[k, n].astype(F32)
            part[k, n] = a
            zsend[k, n] = a.astype(BF16)
        to_mid(k).start()

    def stage_units(k):
        to_mid(k).wait_recv()
        g = part[k, 0] + zin2[k, 0].astype(F32)
        u = part[k, 1] + zin2[k, 1].astype(F32)
        h = part[k, 2] + zin2[k, 2].astype(F32)
        sig = 1.0 / (1.0 + jnp.exp(-g))
        silu = g * sig
        res[k, 0] = (silu * u).astype(BF16)
        res[k, 1] = (h * u * sig * (1.0 + g * (1.0 - sig))).astype(BF16)
        res[k, 2] = (h * silu).astype(BF16)
        to_end(k).start()

    def stage_project(k):
        @pl.when(is_end)
        def _():
            to_end(k).wait_recv()

        hid, gg, ug = res[k, 0], res[k, 1], res[k, 2]
        both[k, 0] = dot_nt(hid, wd[...]).astype(BF16).reshape(both.shape[2:])
        both[k, 1] = (dot_nt(gg, wg[...]) + dot_nt(ug, wu[...])).astype(BF16).reshape(both.shape[2:])
        to_core(k).start()

    def stage_weights(k):
        hid, gg, ug = res[k, 0], res[k, 1], res[k, 2]
        s = slot(k)
        xs = gath[0, s].reshape(rows, feats)
        ys = gath[1, s].reshape(rows, feats)
        d_gate[...] += dot_tn(xs, gg)
        d_up[...] += dot_tn(xs, ug)
        d_down[...] += dot_tn(ys, hid)

    def stage_core(k):
        to_core(k).wait_recv()
        xsend[k] = (both[k, c].astype(F32) + cin[k].astype(F32)).astype(BF16)
        for j in (1, 3, 2):
            scatter_x(k, j).start()

    def stage_x(k):
        for j in (1, 3, 2):
            scatter_x(k, j).wait_recv()
        s = xsend[k, x].astype(F32)
        for j in range(3):
            s += xin[k, j].astype(F32)
        ysend[k] = s.astype(BF16)

        @pl.when(k >= 2)
        def _():
            scatter_y(k).start()

    def step(i, _):
        def when(k, fn, cond=None):
            ok = (k >= 0) & (k < CHUNKS)
            pl.when(ok if cond is None else ok & cond)(lambda: fn(k))

        when(i - 9, stage_x)
        when(i - 7, stage_core)
        when(i - 6, stage_project)
        when(i - 4, stage_units, is_mid)
        when(i - 2, stage_pair, is_mid)
        when(i, stage_partial)
        when(i + 1, stage_forward)

        @pl.when(i == 0)
        def _():
            gather_send(4)
            gather_send(5)

        @pl.when(i == 2)
        def _():
            gather_send(6)
            gather_send(7)

        when(i - 6, stage_weights)
        return 0

    lax.fori_loop(0, CHUNKS + 9, step, 0)

    def total(first, others):
        s = ysend[first].astype(F32)
        for k in others:
            scatter_y(k).wait_recv()
            s += yin[k].astype(F32)
        return s

    zhs[...] = total(1, (4, 5, 6)).astype(BF16)
    half_back().start()
    s = total(0, (2, 3, 7))
    half_back().wait_recv()
    s += zhin[...].astype(F32)
    fin[...] = (gath[c, own, x].astype(F32) + s).astype(BF16)
    last_copy().start()
    last_copy().wait_recv()
    a, b = fin[...].astype(F32), fin_in[...].astype(F32)
    first = jnp.where(c == 0, a[:half], b[half:])
    second = jnp.where(c == 0, b[:half], a[half:])
    out[...] = first.astype(BF16)
    gtok[...] = second.astype(BF16)

    core_copy().wait_send()
    half_copy(own).wait_send()
    for dzh in (0, 1):
        for j in (1, 2, 3):
            gather_x(dzh, j, x).wait_send()

    def drain(k, _):
        @pl.when(k >= 2)
        def _():
            gather_y(k, slot(k), 0).wait_send()
            scatter_y(k).wait_send()

        forward(k, c).wait_send()

        @pl.when(is_end)
        def _():
            to_pair(k).wait_send()

        @pl.when(is_mid)
        def _():
            to_mid(k).wait_send()
            to_end(k).wait_send()

        to_core(k).wait_send()
        for j in (1, 2, 3):
            scatter_x(k, j).wait_send()
        return 0

    lax.fori_loop(0, CHUNKS, drain, 0)
    half_back().wait_send()
    last_copy().wait_send()


def on_device(tokens, gate_weight, up_weight, down_weight, grad_out):
    own_rows, feats = tokens.shape
    units = gate_weight.shape[1]
    block = 2 * own_rows
    rows = 4 * block
    dma = pltpu.SemaphoreType.DMA
    vm = pltpu.VMEM
    wshape = (feats, units)
    any_spec = pl.BlockSpec(memory_space=pl.ANY)
    vmem_spec = pl.BlockSpec(memory_space=pltpu.VMEM)
    return pl.pallas_call(
        body,
        out_shape=(
            jax.ShapeDtypeStruct(tokens.shape, BF16),
            jax.ShapeDtypeStruct(tokens.shape, BF16),
            jax.ShapeDtypeStruct(wshape, F32),
            jax.ShapeDtypeStruct(wshape, F32),
            jax.ShapeDtypeStruct(wshape, F32),
        ),
        in_specs=[vmem_spec, vmem_spec, any_spec, any_spec, any_spec],
        out_specs=[vmem_spec] * 5,
        scratch_shapes=[
            vm(wshape, BF16), vm(wshape, BF16), vm(wshape, BF16),
            vm((block, feats), BF16), vm((block, feats), BF16),
            vm((2, CHUNKS, 4, block, feats), BF16),
            vm((CHUNKS, 3, rows, units), F32),
            vm((CHUNKS, 3, rows, units), BF16),
            vm((CHUNKS, 3, rows, units), BF16),
            vm((CHUNKS, 3, rows, units), BF16),
            vm((CHUNKS, 3, rows, units), BF16),
            vm((CHUNKS, 2, 4, block, feats), BF16),
            vm((CHUNKS, 4, block, feats), BF16),
            vm((CHUNKS, 4, block, feats), BF16),
            vm((CHUNKS, 3, block, feats), BF16),
            vm((CHUNKS, block, feats), BF16),
            vm((CHUNKS, block, feats), BF16),
            vm((block, feats), BF16), vm((block, feats), BF16),
            vm((block, feats), BF16), vm((block, feats), BF16),
            dma((3,)),
            dma((2, 1)), dma((2, 1)), dma((2, 2, 3)), dma((2, CHUNKS)), dma((2, CHUNKS)),
            dma((2, CHUNKS)), dma((2, CHUNKS)), dma((2, CHUNKS)), dma((2, CHUNKS)),
            dma((2, CHUNKS, 3)), dma((2, CHUNKS)), dma((2, 1)), dma((2, 1)),
        ],
        compiler_params=pltpu.CompilerParams(
            collective_id=0, has_side_effects=True, vmem_limit_bytes=60 << 20
        ),
        cost_estimate=pl.CostEstimate(
            flops=18 * 8 * rows * feats * units,
            transcendentals=8 * rows * units,
            bytes_accessed=20 * feats * units,
        ),
        name="swiglu_block",
    )(tokens, grad_out, gate_weight, up_weight, down_weight)


def solution(mesh):
    rows_spec = P(("gx", "gy"), "gz")
    weight_spec = P("gz", ("gx", "gy"))
    return jax.shard_map(
        on_device,
        mesh=mesh,
        in_specs=(rows_spec, weight_spec, weight_spec, weight_spec, rows_spec),
        out_specs=(rows_spec, rows_spec, weight_spec, weight_spec, weight_spec),
        check_vma=False,
    )
```

```python
import functools

import jax
import jax.numpy as jnp
from jax import lax
from jax.experimental import pallas as pl
from jax.experimental.pallas import tpu as pltpu
from jax.sharding import PartitionSpec as P

MESH = pl.DeviceIdType.MESH
F32 = jnp.float32
BF16 = jnp.bfloat16
CHUNKS = 8


def chunk_place(k):
    pair, odd = k // 2, k % 2
    late, last = pair // 2, pair // 3
    dzh = (1 - late) * odd + late - last
    dy = late * (3 - odd) + (pair + 2) // 3 - late
    return dzh, dy


def dot_nn(a, b):
    return jnp.dot(a, b, preferred_element_type=F32)


def dot_nt(a, b):
    return lax.dot_general(a, b, (((1,), (1,)), ((), ())), preferred_element_type=F32)


def dot_tn(a, b):
    return lax.dot_general(a, b, (((0,), (0,)), ((), ())), preferred_element_type=F32)


def body(
    tok, grd, wg_any, wu_any, wd_any,
    out, gtok, d_gate, d_up, d_down,
    wg, wu, wd, mine, theirs, gath, part, zsend, zin1, zin2, res,
    both, cin, xsend, xin, ysend, yin, zhs, zhin, fin, fin_in,
    w_sem, cx, zx, xa, ya, fw, z1, z2, z3, co, xr, yr, zr, fo,
):
    gx, gy, zl = lax.axis_index("gx"), lax.axis_index("gy"), lax.axis_index("gz")
    x, zh, y, c = gx // 2, gx % 2, gy // 2, gy % 2
    units = wg.shape[1]
    feats = wg.shape[0]
    block = gath.shape[3]
    rows = 4 * block

    def at(x_, zh_, y_, c_, zl_):
        return (x_ * 2 + zh_, y_ * 2 + c_, zl_)

    def x_peer(j):
        return at((x + j) % 4, zh, y, c, zl)

    def y_peer(j):
        return at(x, zh, (y + j) % 4, c, zl)

    core_peer = at(x, zh, y, 1 - c, zl)
    half_peer = at(x, 1 - zh, y, c, zl)
    pair_z = zl + 1 - 2 * (zl % 2)
    pair_peer = at(x, zh, y, c, pair_z)
    mid_peer = at(x, zh, y, c, 3 - zl)
    is_mid = ((zl + 1) // 2) % 2 == 1
    is_end = ((zl + 1) // 2) % 2 == 0

    def send(src, dst, sems, idx, peer):
        return pltpu.make_async_remote_copy(
            src_ref=src, dst_ref=dst, send_sem=sems.at[(0, *idx)], recv_sem=sems.at[(1, *idx)],
            device_id=peer, device_id_type=MESH,
        )

    def slot(k):
        dzh, dy = chunk_place(k)
        return ((zh + dzh) % 2) * 4 + (y + dy) % 4

    def column(j):
        return (x + j) % 4

    def core_copy():
        return send(mine, theirs, cx, (0,), core_peer)

    def half_copy(place):
        return send(gath.at[c, place, x], gath.at[c, place, x], zx, (0,), half_peer)

    def gather_x(dzh, j, owner):
        place = ((zh + dzh) % 2) * 4 + y
        return send(gath.at[c, place, owner], gath.at[c, place, owner], xa, (dzh, j - 1), x_peer(-j))

    def gather_y(k, j, place, dy):
        b = column(j)
        return send(gath.at[c, place, b], gath.at[c, place, b], ya, (k, j), y_peer(4 - dy))

    def forward(k, b, which):
        s = slot(k)
        return send(gath.at[which, s, b], gath.at[which, s, b], fw, (k, b), core_peer)

    def to_pair(k, b):
        return send(zsend.at[k, b], zin1.at[k, b], z1, (k, b), pair_peer)

    def to_mid(k, b):
        return send(zsend.at[k, b], zin2.at[k, b], z2, (k, b), mid_peer)

    def to_end(k, b):
        return send(res.at[k, b], res.at[k, b], z3, (k, b), pair_peer)

    def to_core(k):
        return send(both.at[k, 1 - c], cin.at[k], co, (k,), core_peer)

    def scatter_x(k, j):
        return send(xsend.at[k, (x + j) % 4], xin.at[k, j - 1], xr, (k, j - 1), x_peer(j))

    def scatter_y(k):
        _, dy = chunk_place(k)
        return send(ysend.at[k], yin.at[k], yr, (k,), y_peer(dy))

    def half_back():
        return send(zhs, zhin, zr, (0,), half_peer)

    def last_copy():
        return send(fin, fin_in, fo, (0,), core_peer)

    weight_copies = [
        pltpu.make_async_copy(src, dst, w_sem.at[n])
        for n, (src, dst) in enumerate(((wg_any, wg), (wu_any, wu), (wd_any, wd)))
    ]
    for cp in weight_copies:
        cp.start()

    peers = [core_peer, half_peer, pair_peer, mid_peer]
    peers += [x_peer(j) for j in (1, 2, 3)] + [y_peer(j) for j in (1, 2, 3)]
    barrier = pltpu.get_barrier_semaphore()
    for peer in peers:
        pl.semaphore_signal(barrier, inc=1, device_id=peer, device_id_type=MESH)
    mine[...] = jnp.concatenate([tok[...].astype(F32), grd[...].astype(F32)], axis=0).astype(BF16)
    pl.semaphore_wait(barrier, len(peers))

    core_copy().start()
    core_copy().wait_recv()
    m, t = mine[...].astype(F32), theirs[...].astype(F32)
    half = m.shape[0] // 2
    own = zh * 4 + y
    other = (1 - zh) * 4 + y
    for n in range(2):
        mh, th = m[n * half:(n + 1) * half], t[n * half:(n + 1) * half]
        lo = jnp.where(c == 0, mh, th)
        hi = jnp.where(c == 0, th, mh)
        gath[n, own, x] = jnp.concatenate([lo, hi], axis=0).astype(BF16)

    def gather_send(k, j):
        dzh, dy = chunk_place(k)
        gather_y(k, j, ((zh + dzh) % 2) * 4 + y, dy).start()

    half_copy(own).start()
    for j in (1, 3):
        gather_x(0, j, x).start()
    for k in (2, 6):
        gather_send(k, 0)
    gather_x(0, 2, x).start()
    gather_send(7, 0)
    for cp in weight_copies:
        cp.wait()
    for d in (d_gate, d_up, d_down):
        d[...] = jnp.zeros_like(d)

    def block_partial(k, b):
        s = slot(k)
        for n, w in enumerate((wg, wu, wd)):
            p = dot_nn(gath[n // 2, s, b], w[...])
            part[k, b, n] = p
            zsend[k, b, n] = p.astype(BF16)

        @pl.when(is_end)
        def _():
            to_pair(k, b).start()

    def first_pass(k, j):
        if k == 0:
            gather_x(0, j, column(j)).wait_recv()
        else:
            gather_y(k, j, slot(k), 0).wait_recv()
        forward(k, column(j), c).start()

    def first_work(k, j):
        forward(k, column(j), 1 - c).wait_recv()
        block_partial(k, column(j))

    near, far = ((0, 1), (0, 3), (2, 0), (6, 0)), ((0, 2), (7, 0))
    early = ((0, 0),) + near + far
    block_partial(0, x)
    for k, j in near:
        first_pass(k, j)
    for j in (1, 3):
        gather_send(2, j)
        gather_send(6, j)
    for k, j in near:
        first_work(k, j)
    for k, j in far:
        first_pass(k, j)
    gather_send(2, 2)
    gather_send(6, 2)
    for k, j in far:
        first_work(k, j)
    def late(k, j):
        dzh, _ = chunk_place(k)
        return (dzh == 1) | (j != 0)

    def each_late(k, fn):
        for b in range(4):
            pl.when(late(k, b - x))(lambda: fn(b))

    def stage_partial(k):
        each_late(k, lambda b: forward(k, b, 1 - c).wait_recv())
        s = slot(k)
        xs = gath[0, s].reshape(rows, feats)
        ys = gath[1, s].reshape(rows, feats)
        p = [dot_nn(a, w[...]) for a, w in ((xs, wg), (xs, wu), (ys, wd))]

        def keep(b):
            for n in range(3):
                q = p[n][b * block:(b + 1) * block]
                part[k, b, n] = q
                zsend[k, b, n] = q.astype(BF16)

            @pl.when(is_end)
            def _():
                to_pair(k, b).start()

        each_late(k, keep)

    def stage_forward(k):
        @pl.when(k == 1)
        def _():
            for j in (1, 3, 2):
                gather_x(1, j, column(j)).wait_recv()
                forward(k, column(j), c).start()
            for j in (1, 3, 2):
                gather_send(3, j)
                gather_send(4, j)

        @pl.when(k >= 2)
        def _():
            for j in (0, 1, 3, 2):
                @pl.when(late(k, j))
                def _():
                    gather_y(k, j, slot(k), 0).wait_recv()
                    forward(k, column(j), c).start()

        @pl.when(k == 3)
        def _():
            for j in (1, 3, 2):
                gather_send(5, j)
                gather_send(7, j)

    def pair_block(k, b):
        to_pair(k, b).wait_recv()
        for n in range(3):
            a = part[k, b, n] + zin1[k, b, n].astype(F32)
            part[k, b, n] = a
            zsend[k, b, n] = a.astype(BF16)
        to_mid(k, b).start()

    def units_block(k, b):
        to_mid(k, b).wait_recv()
        g, u, h = [part[k, b, n] + zin2[k, b, n].astype(F32) for n in range(3)]
        sig = 1.0 / (1.0 + jnp.exp(-g))
        silu = g * sig
        res[k, b, 0] = (silu * u).astype(BF16)
        res[k, b, 1] = (h * u * sig * (1.0 + g * (1.0 - sig))).astype(BF16)
        res[k, b, 2] = (h * silu).astype(BF16)
        to_end(k, b).start()

    def take(*work):
        for fn, (k, j) in work:
            fn(k, column(j))

    first = early

    def stage_mid(i):
        @pl.when(i == 1)
        def _():
            for n in (4, 5, 6):
                take((pair_block, first[n]), (units_block, first[n - 3]))

        @pl.when(i == 2)
        def _():
            for n in (4, 5, 6):
                pair_block(1, n - 4)
                take((units_block, first[n]))
            pair_block(1, 3)

        @pl.when(i >= 3)
        def _():
            for b in range(4):
                @pl.when((i <= CHUNKS) & late(i - 1, b - x))
                def _():
                    pair_block(i - 1, b)

                @pl.when((i <= CHUNKS + 1) & late(i - 2, b - x))
                def _():
                    units_block(i - 2, b)

    def results(k):
        return [res[k, :, n].reshape(rows, units) for n in range(3)]

    def stage_project(k):
        @pl.when(is_end)
        def _():
            for b in range(4):
                to_end(k, b).wait_recv()

        hid, gg, ug = results(k)
        both[k, 0] = dot_nt(hid, wd[...]).astype(BF16).reshape(both.shape[2:])
        both[k, 1] = (dot_nt(gg, wg[...]) + dot_nt(ug, wu[...])).astype(BF16).reshape(both.shape[2:])
        to_core(k).start()

    def stage_weights(k):
        hid, gg, ug = results(k)
        s = slot(k)
        xs = gath[0, s].reshape(rows, feats)
        ys = gath[1, s].reshape(rows, feats)
        d_gate[...] += dot_tn(xs, gg)
        d_up[...] += dot_tn(xs, ug)
        d_down[...] += dot_tn(ys, hid)

    def stage_core(k):
        to_core(k).wait_recv()
        xsend[k] = (both[k, c].astype(F32) + cin[k].astype(F32)).astype(BF16)
        for j in (1, 3, 2):
            scatter_x(k, j).start()

    def stage_x(k):
        for j in (1, 3, 2):
            scatter_x(k, j).wait_recv()
        s = xsend[k, x].astype(F32)
        for j in range(3):
            s += xin[k, j].astype(F32)
        ysend[k] = s.astype(BF16)

        @pl.when(k >= 2)
        def _():
            scatter_y(k).start()

    @pl.when(is_mid)
    def _():
        take((pair_block, first[0]))

    half_copy(other).wait_recv()
    forward(1, x, c).start()
    for j in (1, 3, 2):
        gather_x(1, j, x).start()
    for k in (3, 4, 5):
        gather_send(k, 0)

    @pl.when(is_mid)
    def _():
        take((units_block, first[0]))
        for n in (1, 2, 3):
            take((pair_block, first[n]))

    stage_forward(1)

    def step(i, _):
        def when(k, fn, cond=None):
            ok = (k >= 0) & (k < CHUNKS)
            pl.when(ok if cond is None else ok & cond)(lambda: fn(k))

        pl.when(is_mid)(lambda: stage_mid(i))
        when(i, stage_partial)
        when(i + 1, stage_forward)
        when(i - 7, stage_x)
        when(i - 5, stage_core)
        when(i - 4, stage_project)
        when(i - 4, stage_weights)
        return 0

    lax.fori_loop(1, CHUNKS + 3, step, 0)
    stage_x(4)
    stage_core(6)
    stage_x(5)
    stage_project(7)
    stage_weights(7)
    stage_core(7)

    def total(first, others):
        s = ysend[first].astype(F32)
        for k in others:
            scatter_y(k).wait_recv()
            s += yin[k].astype(F32)
        return s

    stage_x(6)
    zhs[...] = total(1, (3, 4, 5)).astype(BF16)
    half_back().start()
    stage_x(7)
    s = total(0, (2, 6, 7))
    half_back().wait_recv()
    s += zhin[...].astype(F32)
    fin[...] = (gath[c, own, x].astype(F32) + s).astype(BF16)
    last_copy().start()
    last_copy().wait_recv()
    a, b = fin[...].astype(F32), fin_in[...].astype(F32)
    first = jnp.where(c == 0, a[:half], b[half:])
    second = jnp.where(c == 0, b[:half], a[half:])
    out[...] = first.astype(BF16)
    gtok[...] = second.astype(BF16)

    core_copy().wait_send()
    half_copy(own).wait_send()
    for dzh in (0, 1):
        for j in (1, 2, 3):
            gather_x(dzh, j, x).wait_send()

    def drain(k, _):
        @pl.when(k >= 2)
        def _():
            for j in range(4):
                gather_y(k, j, slot(k), 0).wait_send()
            scatter_y(k).wait_send()

        for b in range(4):
            @pl.when((k != 0) | (b != x))
            def _():
                forward(k, b, c).wait_send()

            @pl.when(is_end)
            def _():
                to_pair(k, b).wait_send()

            @pl.when(is_mid)
            def _():
                to_mid(k, b).wait_send()
                to_end(k, b).wait_send()

        to_core(k).wait_send()
        for j in (1, 2, 3):
            scatter_x(k, j).wait_send()
        return 0

    lax.fori_loop(0, CHUNKS, drain, 0)
    half_back().wait_send()
    last_copy().wait_send()


def on_device(tokens, gate_weight, up_weight, down_weight, grad_out):
    own_rows, feats = tokens.shape
    units = gate_weight.shape[1]
    block = 2 * own_rows
    rows = 4 * block
    dma = pltpu.SemaphoreType.DMA
    vm = pltpu.VMEM
    wshape = (feats, units)
    any_spec = pl.BlockSpec(memory_space=pl.ANY)
    vmem_spec = pl.BlockSpec(memory_space=pltpu.VMEM)
    return pl.pallas_call(
        body,
        out_shape=(
            jax.ShapeDtypeStruct(tokens.shape, BF16),
            jax.ShapeDtypeStruct(tokens.shape, BF16),
            jax.ShapeDtypeStruct(wshape, F32),
            jax.ShapeDtypeStruct(wshape, F32),
            jax.ShapeDtypeStruct(wshape, F32),
        ),
        in_specs=[vmem_spec, vmem_spec, any_spec, any_spec, any_spec],
        out_specs=[vmem_spec] * 5,
        scratch_shapes=[
            vm(wshape, BF16), vm(wshape, BF16), vm(wshape, BF16),
            vm((block, feats), BF16), vm((block, feats), BF16),
            vm((2, CHUNKS, 4, block, feats), BF16),
            vm((CHUNKS, 4, 3, block, units), F32),
            vm((CHUNKS, 4, 3, block, units), BF16),
            vm((CHUNKS, 4, 3, block, units), BF16),
            vm((CHUNKS, 4, 3, block, units), BF16),
            vm((CHUNKS, 4, 3, block, units), BF16),
            vm((CHUNKS, 2, 4, block, feats), BF16),
            vm((CHUNKS, 4, block, feats), BF16),
            vm((CHUNKS, 4, block, feats), BF16),
            vm((CHUNKS, 3, block, feats), BF16),
            vm((CHUNKS, block, feats), BF16),
            vm((CHUNKS, block, feats), BF16),
            vm((block, feats), BF16), vm((block, feats), BF16),
            vm((block, feats), BF16), vm((block, feats), BF16),
            dma((3,)),
            dma((2, 1)), dma((2, 1)), dma((2, 2, 3)), dma((2, CHUNKS, 4)), dma((2, CHUNKS, 4)),
            dma((2, CHUNKS, 4)), dma((2, CHUNKS, 4)), dma((2, CHUNKS, 4)), dma((2, CHUNKS)),
            dma((2, CHUNKS, 3)), dma((2, CHUNKS)), dma((2, 1)), dma((2, 1)),
        ],
        compiler_params=pltpu.CompilerParams(
            collective_id=0, has_side_effects=True, vmem_limit_bytes=60 << 20
        ),
        cost_estimate=pl.CostEstimate(
            flops=18 * 8 * rows * feats * units,
            transcendentals=8 * rows * units,
            bytes_accessed=20 * feats * units,
        ),
        name="swiglu_block",
    )(tokens, grad_out, gate_weight, up_weight, down_weight)


def solution(mesh):
    rows_spec = P(("gx", "gy"), "gz")
    weight_spec = P("gz", ("gx", "gy"))
    return jax.shard_map(
        on_device,
        mesh=mesh,
        in_specs=(rows_spec, weight_spec, weight_spec, weight_spec, rows_spec),
        out_specs=(rows_spec, rows_spec, weight_spec, weight_spec, weight_spec),
        check_vma=False,
    )
```

```python
import functools

import jax
import jax.numpy as jnp
from jax import lax
from jax.experimental import pallas as pl
from jax.experimental.pallas import tpu as pltpu
from jax.sharding import PartitionSpec as P

MESH = pl.DeviceIdType.MESH
F32 = jnp.float32
BF16 = jnp.bfloat16
CHUNKS = 8
LAST_OWN = (1, 3, 2, 0)


def chunk_place(k):
    pair, odd = k // 2, k % 2
    late, last = pair // 2, pair // 3
    dzh = (1 - late) * odd + late - last
    dy = late * (3 - odd) + (pair + 2) // 3 - late
    return dzh, dy


def dot_nn(a, b):
    return jnp.dot(a, b, preferred_element_type=F32)


def dot_tn(a, b):
    return lax.dot_general(a, b, (((0,), (0,)), ((), ())), preferred_element_type=F32)


def body(
    tok_any, grd_any, wg_any, wu_any, wd_any,
    out, gtok, d_gate, d_up, d_down,
    tok, grd, wg, wu, wd, wgt, wut, wdt, mine, theirs, gath, part, zsend, zin1, zin2, res,
    both, cin, xsend, xin, ysend, yin, zhs, zhin, fin, fin_in,
    w_sem, cx, zx, xa, ya, fw, z1, z2, z3, co, cl, xr, yr, zr, fo,
):
    gx, gy, zl = lax.axis_index("gx"), lax.axis_index("gy"), lax.axis_index("gz")
    x, zh, y, c = gx // 2, gx % 2, gy // 2, gy % 2
    units = wg.shape[1]
    feats = wg.shape[0]
    block = gath.shape[3]
    rows = 4 * block

    def at(x_, zh_, y_, c_, zl_):
        return (x_ * 2 + zh_, y_ * 2 + c_, zl_)

    def x_peer(j):
        return at((x + j) % 4, zh, y, c, zl)

    def y_peer(j):
        return at(x, zh, (y + j) % 4, c, zl)

    core_peer = at(x, zh, y, 1 - c, zl)
    half_peer = at(x, 1 - zh, y, c, zl)
    pair_z = zl + 1 - 2 * (zl % 2)
    pair_peer = at(x, zh, y, c, pair_z)
    mid_peer = at(x, zh, y, c, 3 - zl)
    is_mid = ((zl + 1) // 2) % 2 == 1
    is_end = ((zl + 1) // 2) % 2 == 0

    def send(src, dst, sems, idx, peer):
        return pltpu.make_async_remote_copy(
            src_ref=src, dst_ref=dst, send_sem=sems.at[(0, *idx)], recv_sem=sems.at[(1, *idx)],
            device_id=peer, device_id_type=MESH,
        )

    def slot(k):
        dzh, dy = chunk_place(k)
        return ((zh + dzh) % 2) * 4 + (y + dy) % 4

    def column(j):
        return (x + j) % 4

    def core_copy():
        return send(mine, theirs, cx, (0,), core_peer)

    def half_copy(place):
        return send(gath.at[c, place, x], gath.at[c, place, x], zx, (0,), half_peer)

    def gather_x(dzh, j, owner):
        place = ((zh + dzh) % 2) * 4 + y
        return send(gath.at[c, place, owner], gath.at[c, place, owner], xa, (dzh, j - 1), x_peer(-j))

    def gather_y(k, j, place, dy):
        b = column(j)
        return send(gath.at[c, place, b], gath.at[c, place, b], ya, (k, j), y_peer(4 - dy))

    def forward(k, b, which):
        s = slot(k)
        return send(gath.at[which, s, b], gath.at[which, s, b], fw, (k, b), core_peer)

    def to_pair(k, b):
        return send(zsend.at[k, b], zin1.at[k, b], z1, (k, b), pair_peer)

    def to_mid(k, b):
        return send(zsend.at[k, b], zin2.at[k, b], z2, (k, b), mid_peer)

    def to_end(k, b):
        return send(res.at[k, b], res.at[k, b], z3, (k, b), pair_peer)

    def to_core(k):
        return send(both.at[k, 1 - c], cin.at[k], co, (k,), core_peer)

    def last_core(b):
        return send(both.at[CHUNKS - 1, 1 - c, b], cin.at[CHUNKS - 1, b], cl, (b,), core_peer)

    def scatter_x(k, j):
        return send(xsend.at[k, (x + j) % 4], xin.at[k, j - 1], xr, (k, j - 1), x_peer(j))

    def scatter_y(k):
        _, dy = chunk_place(k)
        return send(ysend.at[k], yin.at[k], yr, (k,), y_peer(dy))

    def half_back():
        return send(zhs, zhin, zr, (0,), half_peer)

    def last_copy():
        return send(fin, fin_in, fo, (0,), core_peer)

    weight_copies = [
        pltpu.make_async_copy(src, dst, w_sem.at[n])
        for n, (src, dst) in enumerate(((wg_any, wg), (wu_any, wu), (wd_any, wd)))
    ]
    row_copies = [pltpu.make_async_copy(tok_any, tok, w_sem.at[3]), pltpu.make_async_copy(grd_any, grd, w_sem.at[4])]
    for cp in row_copies + weight_copies:
        cp.start()

    peers = [core_peer, half_peer, pair_peer, mid_peer]
    peers += [x_peer(j) for j in (1, 2, 3)] + [y_peer(j) for j in (1, 2, 3)]
    barrier = pltpu.get_barrier_semaphore()
    for peer in peers:
        pl.semaphore_signal(barrier, inc=1, device_id=peer, device_id_type=MESH)
    for cp in row_copies:
        cp.wait()
    mine[...] = jnp.concatenate([tok[...].astype(F32), grd[...].astype(F32)], axis=0).astype(BF16)
    pl.semaphore_wait(barrier, len(peers))

    core_copy().start()
    core_copy().wait_recv()
    m, t = mine[...].astype(F32), theirs[...].astype(F32)
    half = m.shape[0] // 2
    own = zh * 4 + y
    other = (1 - zh) * 4 + y
    for n in range(2):
        mh, th = m[n * half:(n + 1) * half], t[n * half:(n + 1) * half]
        lo = jnp.where(c == 0, mh, th)
        hi = jnp.where(c == 0, th, mh)
        gath[n, own, x] = jnp.concatenate([lo, hi], axis=0).astype(BF16)

    def gather_send(k, j):
        dzh, dy = chunk_place(k)
        gather_y(k, j, ((zh + dzh) % 2) * 4 + y, dy).start()

    half_copy(own).start()
    for j in (1, 3):
        gather_x(0, j, x).start()
    for k in (2, 6):
        gather_send(k, 0)
    gather_x(0, 2, x).start()
    for cp in weight_copies:
        cp.wait()
    for d in (d_gate, d_up, d_down):
        d[...] = jnp.zeros_like(d)

    def block_partial(k, b):
        s = slot(k)
        for n, w in enumerate((wg, wu, wd)):
            p = dot_nn(gath[n // 2, s, b], w[...])
            part[k, b, n] = p
            zsend[k, b, n] = p.astype(BF16)

        @pl.when(is_end)
        def _():
            to_pair(k, b).start()

    def first_pass(k, j):
        if k == 0:
            gather_x(0, j, column(j)).wait_recv()
        else:
            gather_y(k, j, slot(k), 0).wait_recv()
        forward(k, column(j), c).start()

    def first_work(k, j):
        forward(k, column(j), 1 - c).wait_recv()
        block_partial(k, column(j))

    near, far = ((0, 1), (0, 3), (2, 0), (6, 0)), ((0, 2),)
    early = ((0, 0),) + near + far
    block_partial(0, x)
    for flat, turned in ((wg, wgt), (wu, wut), (wd, wdt)):
        turned[...] = flat[...].T
    for k, j in near:
        first_pass(k, j)
    for j in (1, 3):
        gather_send(2, j)
        gather_send(6, j)
    for k, j in near:
        first_work(k, j)
    for k, j in far:
        first_pass(k, j)
    gather_send(2, 2)
    gather_send(6, 2)
    for k, j in far:
        first_work(k, j)
    def late(k, j):
        dzh, _ = chunk_place(k)
        return (dzh == 1) | (j != 0) | (k == CHUNKS - 1)

    def each_late(k, fn):
        for j in LAST_OWN:
            pl.when(late(k, j))(lambda: fn(column(j)))

    def stage_partial(k):
        each_late(k, lambda b: forward(k, b, 1 - c).wait_recv())
        s = slot(k)
        xs = gath[0, s].reshape(rows, feats)
        ys = gath[1, s].reshape(rows, feats)
        p = [dot_nn(a, w[...]) for a, w in ((xs, wg), (xs, wu), (ys, wd))]

        for b in range(4):
            @pl.when(late(k, b - x))
            def _():
                for n in range(3):
                    q = p[n][b * block:(b + 1) * block]
                    part[k, b, n] = q
                    zsend[k, b, n] = q.astype(BF16)

        @pl.when(is_end)
        def _():
            each_late(k, lambda b: to_pair(k, b).start())

    def stage_forward(k):
        @pl.when(k == 1)
        def _():
            for j in (1, 3, 2):
                gather_x(1, j, column(j)).wait_recv()
                forward(k, column(j), c).start()
            for j in (1, 3, 2):
                gather_send(3, j)
                gather_send(4, j)

        @pl.when(k >= 2)
        def _():
            for j in LAST_OWN:
                @pl.when(late(k, j))
                def _():
                    gather_y(k, j, slot(k), 0).wait_recv()
                    forward(k, column(j), c).start()

        @pl.when(k == 3)
        def _():
            for j in LAST_OWN:
                if j:
                    gather_send(5, j)
                gather_send(7, j)

    def pair_block(k, b):
        to_pair(k, b).wait_recv()
        for n in range(3):
            a = part[k, b, n] + zin1[k, b, n].astype(F32)
            part[k, b, n] = a
            zsend[k, b, n] = a.astype(BF16)
        to_mid(k, b).start()

    def units_block(k, b):
        to_mid(k, b).wait_recv()
        g, u, h = [part[k, b, n] + zin2[k, b, n].astype(F32) for n in range(3)]
        sig = 1.0 / (1.0 + jnp.exp(-g))
        silu = g * sig
        res[k, b, 0] = (silu * u).astype(BF16)
        res[k, b, 1] = (h * u * sig * (1.0 + g * (1.0 - sig))).astype(BF16)
        res[k, b, 2] = (h * silu).astype(BF16)
        to_end(k, b).start()

    def take(*work):
        for fn, (k, j) in work:
            fn(k, column(j))

    first = early

    def stage_mid(i):
        @pl.when(i == 1)
        def _():
            for n in (4, 5):
                take((pair_block, first[n]), (units_block, first[n - 3]))

        @pl.when(i == 2)
        def _():
            for n in (3, 4, 5):
                take((pair_block, (1, LAST_OWN[n - 3])), (units_block, first[n]))
            take((pair_block, (1, LAST_OWN[3])))

        @pl.when(i >= 3)
        def _():
            for j in LAST_OWN:
                @pl.when((i <= CHUNKS) & late(i - 1, j))
                def _():
                    pair_block(i - 1, column(j))

                @pl.when((i <= CHUNKS + 1) & late(i - 2, j))
                def _():
                    units_block(i - 2, column(j))

    def results(k):
        return [res[k, :, n].reshape(rows, units) for n in range(3)]

    def stage_project(k):
        @pl.when(is_end)
        def _():
            for b in range(4):
                to_end(k, b).wait_recv()

        hid, gg, ug = results(k)
        both[k, 0] = dot_nn(hid, wdt[...]).astype(BF16).reshape(both.shape[2:])
        both[k, 1] = (dot_nn(gg, wgt[...]) + dot_nn(ug, wut[...])).astype(BF16).reshape(both.shape[2:])
        to_core(k).start()

    def stage_weights(k):
        hid, gg, ug = results(k)
        s = slot(k)
        xs = gath[0, s].reshape(rows, feats)
        ys = gath[1, s].reshape(rows, feats)
        d_gate[...] += dot_tn(xs, gg)
        d_up[...] += dot_tn(xs, ug)
        d_down[...] += dot_tn(ys, hid)

    def stage_core(k):
        to_core(k).wait_recv()
        xsend[k] = (both[k, c].astype(F32) + cin[k].astype(F32)).astype(BF16)
        for j in (1, 3, 2):
            scatter_x(k, j).start()

    def stage_x(k):
        for j in (1, 3, 2):
            scatter_x(k, j).wait_recv()
        s = xsend[k, x].astype(F32)
        for j in range(3):
            s += xin[k, j].astype(F32)
        ysend[k] = s.astype(BF16)

        @pl.when(k >= 2)
        def _():
            scatter_y(k).start()

    @pl.when(is_mid)
    def _():
        take((pair_block, first[0]))

    half_copy(other).wait_recv()
    forward(1, x, c).start()
    for j in (1, 3, 2):
        gather_x(1, j, x).start()
    for k in (3, 4, 5):
        gather_send(k, 0)

    @pl.when(is_mid)
    def _():
        take((units_block, first[0]))
        for n in (1, 2, 3):
            take((pair_block, first[n]))

    stage_forward(1)

    def step(i, _):
        def when(k, fn, cond=None):
            ok = (k >= 0) & (k < CHUNKS)
            pl.when(ok if cond is None else ok & cond)(lambda: fn(k))

        pl.when(is_mid)(lambda: stage_mid(i))
        when(i, stage_partial)
        when(i + 1, stage_forward)
        when(i - 7, stage_x)
        when(i - 5, stage_core)
        when(i - 4, stage_project)
        when(i - 4, stage_weights)
        return 0

    lax.fori_loop(1, CHUNKS + 3, step, 0)
    def total(first, others):
        s = ysend[first].astype(F32)
        for k in others:
            scatter_y(k).wait_recv()
            s += yin[k].astype(F32)
        return s

    end = CHUNKS - 1

    def last_project(j):
        b = column(j)

        @pl.when(is_end)
        def _():
            to_end(end, b).wait_recv()

        hid, gg, ug = res[end, b, 0], res[end, b, 1], res[end, b, 2]
        both[end, 0, b] = dot_nn(hid, wdt[...]).astype(BF16)
        both[end, 1, b] = (dot_nn(gg, wgt[...]) + dot_nn(ug, wut[...])).astype(BF16)
        last_core(b).start()

    def last_scatter(j):
        b = column(j)
        last_core(b).wait_recv()
        xsend[end, b] = (both[end, c, b].astype(F32) + cin[end, b].astype(F32)).astype(BF16)
        if j:
            scatter_x(end, j).start()

    stage_core(6)
    stage_x(4)
    last_project(1)
    last_project(3)
    last_scatter(1)
    stage_x(5)
    last_project(2)
    last_scatter(3)
    last_project(0)
    last_scatter(2)
    last_scatter(0)
    stage_x(6)
    zhs[...] = total(1, (3, 4, 5)).astype(BF16)
    half_back().start()
    stage_x(end)
    stage_weights(end)
    s = total(0, (2, 6, 7))
    half_back().wait_recv()
    s += zhin[...].astype(F32)
    fin[...] = (gath[c, own, x].astype(F32) + s).astype(BF16)
    last_copy().start()
    last_copy().wait_recv()
    a, b = fin[...].astype(F32), fin_in[...].astype(F32)
    first = jnp.where(c == 0, a[:half], b[half:])
    second = jnp.where(c == 0, b[:half], a[half:])
    out[...] = first.astype(BF16)
    gtok[...] = second.astype(BF16)

    core_copy().wait_send()
    half_copy(own).wait_send()
    for dzh in (0, 1):
        for j in (1, 2, 3):
            gather_x(dzh, j, x).wait_send()

    def drain(k, _):
        @pl.when(k >= 2)
        def _():
            for j in range(4):
                gather_y(k, j, slot(k), 0).wait_send()
            scatter_y(k).wait_send()

        for b in range(4):
            @pl.when((k != 0) | (b != x))
            def _():
                forward(k, b, c).wait_send()

            @pl.when(is_end)
            def _():
                to_pair(k, b).wait_send()

            @pl.when(is_mid)
            def _():
                to_mid(k, b).wait_send()
                to_end(k, b).wait_send()

        @pl.when(k < CHUNKS - 1)
        def _():
            to_core(k).wait_send()

        for j in (1, 2, 3):
            scatter_x(k, j).wait_send()
        return 0

    lax.fori_loop(0, CHUNKS, drain, 0)
    for b in range(4):
        last_core(b).wait_send()
    half_back().wait_send()
    last_copy().wait_send()


def hand_over(*refs):
    n = (len(refs) - 1) // 2
    sems = refs[-1]
    copies = [pltpu.make_async_copy(refs[i], refs[n + i], sems.at[i]) for i in range(n)]
    for cp in copies:
        cp.start()
    for cp in copies:
        cp.wait()


def on_device(tokens, gate_weight, up_weight, down_weight, grad_out):
    own_rows, feats = tokens.shape
    units = gate_weight.shape[1]
    block = 2 * own_rows
    rows = 4 * block
    dma = pltpu.SemaphoreType.DMA
    vm = pltpu.VMEM
    wshape = (feats, units)
    outs = [(tokens.shape, BF16)] * 2 + [(wshape, F32)] * 3
    any_spec = pl.BlockSpec(memory_space=pl.ANY)
    vmem_spec = pl.BlockSpec(memory_space=pltpu.VMEM)
    made = pl.pallas_call(
        body,
        out_shape=[vm(sh, dt) for sh, dt in outs],
        in_specs=[pl.BlockSpec(memory_space=pltpu.HBM)] * 5,
        out_specs=[vmem_spec] * 5,
        scratch_shapes=[
            vm(tokens.shape, BF16), vm(tokens.shape, BF16),
            vm(wshape, BF16), vm(wshape, BF16), vm(wshape, BF16),
            vm(wshape[::-1], BF16), vm(wshape[::-1], BF16), vm(wshape[::-1], BF16),
            vm((block, feats), BF16), vm((block, feats), BF16),
            vm((2, CHUNKS, 4, block, feats), BF16),
            vm((CHUNKS, 4, 3, block, units), F32),
            vm((CHUNKS, 4, 3, block, units), BF16),
            vm((CHUNKS, 4, 3, block, units), BF16),
            vm((CHUNKS, 4, 3, block, units), BF16),
            vm((CHUNKS, 4, 3, block, units), BF16),
            vm((CHUNKS, 2, 4, block, feats), BF16),
            vm((CHUNKS, 4, block, feats), BF16),
            vm((CHUNKS, 4, block, feats), BF16),
            vm((CHUNKS, 3, block, feats), BF16),
            vm((CHUNKS, block, feats), BF16),
            vm((CHUNKS, block, feats), BF16),
            vm((block, feats), BF16), vm((block, feats), BF16),
            vm((block, feats), BF16), vm((block, feats), BF16),
            dma((5,)),
            dma((2, 1)), dma((2, 1)), dma((2, 2, 3)), dma((2, CHUNKS, 4)), dma((2, CHUNKS, 4)),
            dma((2, CHUNKS, 4)), dma((2, CHUNKS, 4)), dma((2, CHUNKS, 4)), dma((2, CHUNKS)),
            dma((2, 4)), dma((2, CHUNKS, 3)), dma((2, CHUNKS)), dma((2, 1)), dma((2, 1)),
        ],
        compiler_params=pltpu.CompilerParams(
            collective_id=0, has_side_effects=True, vmem_limit_bytes=46 << 20
        ),
        cost_estimate=pl.CostEstimate(
            flops=18 * 8 * rows * feats * units,
            transcendentals=8 * rows * units,
            bytes_accessed=20 * feats * units,
        ),
        name="swiglu_block",
    )(*[
        pltpu.with_memory_space_constraint(a, pltpu.HBM)
        for a in (tokens, grad_out, gate_weight, up_weight, down_weight)
    ])
    return pl.pallas_call(
        hand_over,
        out_shape=[jax.ShapeDtypeStruct(sh, dt) for sh, dt in outs],
        in_specs=[vmem_spec] * len(outs),
        out_specs=[any_spec] * len(outs),
        scratch_shapes=[dma((len(outs),))],
        compiler_params=pltpu.CompilerParams(vmem_limit_bytes=1 << 20),
        name="hand_over",
    )(*made)


def solution(mesh):
    rows_spec = P(("gx", "gy"), "gz")
    weight_spec = P("gz", ("gx", "gy"))
    return jax.shard_map(
        on_device,
        mesh=mesh,
        in_specs=(rows_spec, weight_spec, weight_spec, weight_spec, rows_spec),
        out_specs=(rows_spec, rows_spec, weight_spec, weight_spec, weight_spec),
        check_vma=False,
    )
```

```python
import functools

import jax
import jax.numpy as jnp
from jax import lax
from jax.experimental import pallas as pl
from jax.experimental.pallas import tpu as pltpu
from jax.sharding import PartitionSpec as P

MESH = pl.DeviceIdType.MESH
F32 = jnp.float32
BF16 = jnp.bfloat16
CHUNKS = 8
LAST_OWN = (1, 3, 2, 0)


def chunk_place(k):
    pair, odd = k // 2, k % 2
    late, last = pair // 2, pair // 3
    dzh = (1 - late) * odd + late - last
    dy = late * (3 - odd) + (pair + 2) // 3 - late
    return dzh, dy


def dot_nn(a, b):
    return jnp.dot(a, b, preferred_element_type=F32)


def dot_tn(a, b):
    return lax.dot_general(a, b, (((0,), (0,)), ((), ())), preferred_element_type=F32)


def body(
    tok_any, grd_any, wg_any, wu_any, wd_any,
    out, gtok, d_gate, d_up, d_down,
    tok, grd, wg, wu, wd, wgt, wut, wdt, mine, theirs, gath, part, zsend, zin1, zin2, res,
    both, cin, xsend, xin, ysend, yin, zhs, zhin, fin, fin_in,
    w_sem, cx, zx, xa, ya, fw, z1, z2, z3, co, cl, xr, yr, zr, fo,
):
    gx, gy, zl = lax.axis_index("gx"), lax.axis_index("gy"), lax.axis_index("gz")
    x, zh, y, c = gx // 2, gx % 2, gy // 2, gy % 2
    units = wg.shape[1]
    feats = wg.shape[0]
    block = gath.shape[3]
    rows = 4 * block

    def at(x_, zh_, y_, c_, zl_):
        return (x_ * 2 + zh_, y_ * 2 + c_, zl_)

    def x_peer(j):
        return at((x + j) % 4, zh, y, c, zl)

    def y_peer(j):
        return at(x, zh, (y + j) % 4, c, zl)

    core_peer = at(x, zh, y, 1 - c, zl)
    half_peer = at(x, 1 - zh, y, c, zl)
    pair_z = zl + 1 - 2 * (zl % 2)
    pair_peer = at(x, zh, y, c, pair_z)
    mid_peer = at(x, zh, y, c, 3 - zl)
    is_mid = ((zl + 1) // 2) % 2 == 1
    is_end = ((zl + 1) // 2) % 2 == 0

    def send(src, dst, sems, idx, peer):
        return pltpu.make_async_remote_copy(
            src_ref=src, dst_ref=dst, send_sem=sems.at[(0, *idx)], recv_sem=sems.at[(1, *idx)],
            device_id=peer, device_id_type=MESH,
        )

    def slot(k):
        dzh, dy = chunk_place(k)
        return ((zh + dzh) % 2) * 4 + (y + dy) % 4

    def column(j):
        return (x + j) % 4

    def core_copy():
        return send(mine, theirs, cx, (0,), core_peer)

    def half_copy(place):
        return send(gath.at[c, place, x], gath.at[c, place, x], zx, (0,), half_peer)

    def gather_x(dzh, j, owner):
        place = ((zh + dzh) % 2) * 4 + y
        return send(gath.at[c, place, owner], gath.at[c, place, owner], xa, (dzh, j - 1), x_peer(-j))

    def gather_y(k, j, place, dy):
        b = column(j)
        return send(gath.at[c, place, b], gath.at[c, place, b], ya, (k, j), y_peer(4 - dy))

    def forward(k, b, which):
        s = slot(k)
        return send(gath.at[which, s, b], gath.at[which, s, b], fw, (k, b), core_peer)

    def to_pair(k, b):
        return send(zsend.at[k, b], zin1.at[k, b], z1, (k, b), pair_peer)

    def to_mid(k, b):
        return send(zsend.at[k, b], zin2.at[k, b], z2, (k, b), mid_peer)

    def to_end(k, b):
        return send(res.at[k, b], res.at[k, b], z3, (k, b), pair_peer)

    def to_core(k):
        return send(both.at[k, 1 - c], cin.at[k], co, (k,), core_peer)

    def last_core(b):
        return send(both.at[CHUNKS - 1, 1 - c, b], cin.at[CHUNKS - 1, b], cl, (b,), core_peer)

    def scatter_x(k, j):
        return send(xsend.at[k, (x + j) % 4], xin.at[k, j - 1], xr, (k, j - 1), x_peer(j))

    def scatter_y(k):
        _, dy = chunk_place(k)
        return send(ysend.at[k], yin.at[k], yr, (k,), y_peer(dy))

    def half_back():
        return send(zhs, zhin, zr, (0,), half_peer)

    def last_copy():
        return send(fin, fin_in, fo, (0,), core_peer)

    weight_copies = [
        pltpu.make_async_copy(src, dst, w_sem.at[n])
        for n, (src, dst) in enumerate(((wg_any, wg), (wu_any, wu), (wd_any, wd)))
    ]
    row_copies = [pltpu.make_async_copy(tok_any, tok, w_sem.at[3]), pltpu.make_async_copy(grd_any, grd, w_sem.at[4])]
    for cp in row_copies + weight_copies:
        cp.start()

    peers = [core_peer, half_peer, pair_peer, mid_peer]
    peers += [x_peer(j) for j in (1, 2, 3)] + [y_peer(j) for j in (1, 2, 3)]
    barrier = pltpu.get_barrier_semaphore()
    for peer in peers:
        pl.semaphore_signal(barrier, inc=1, device_id=peer, device_id_type=MESH)
    for cp in row_copies:
        cp.wait()
    mine[...] = jnp.concatenate([tok[...].astype(F32), grd[...].astype(F32)], axis=0).astype(BF16)
    pl.semaphore_wait(barrier, len(peers))

    core_copy().start()
    core_copy().wait_recv()
    m, t = mine[...].astype(F32), theirs[...].astype(F32)
    half = m.shape[0] // 2
    own = zh * 4 + y
    other = (1 - zh) * 4 + y
    for n in range(2):
        mh, th = m[n * half:(n + 1) * half], t[n * half:(n + 1) * half]
        lo = jnp.where(c == 0, mh, th)
        hi = jnp.where(c == 0, th, mh)
        gath[n, own, x] = jnp.concatenate([lo, hi], axis=0).astype(BF16)

    def gather_send(k, j):
        dzh, dy = chunk_place(k)
        gather_y(k, j, ((zh + dzh) % 2) * 4 + y, dy).start()

    half_copy(own).start()
    for j in (1, 3):
        gather_x(0, j, x).start()
    for k in (2, 6):
        gather_send(k, 0)
    gather_x(0, 2, x).start()
    for cp in weight_copies:
        cp.wait()
    for d in (d_gate, d_up, d_down):
        d[...] = jnp.zeros_like(d)

    def block_partial(k, b):
        s = slot(k)
        for n, w in enumerate((wg, wu, wd)):
            p = dot_nn(gath[n // 2, s, b], w[...])
            part[k, b, n] = p
            zsend[k, b, n] = p.astype(BF16)

        @pl.when(is_end)
        def _():
            to_pair(k, b).start()

    def first_pass(k, j):
        if k == 0:
            gather_x(0, j, column(j)).wait_recv()
        else:
            gather_y(k, j, slot(k), 0).wait_recv()
        forward(k, column(j), c).start()

    def first_work(k, j):
        forward(k, column(j), 1 - c).wait_recv()
        block_partial(k, column(j))

    near, far = ((0, 1), (0, 3), (2, 0), (6, 0)), ((0, 2),)
    early = ((0, 0),) + near + far
    block_partial(0, x)
    for flat, turned in ((wg, wgt), (wu, wut), (wd, wdt)):
        turned[...] = flat[...].T
    for k, j in near:
        first_pass(k, j)
    for j in (1, 3):
        gather_send(2, j)
        gather_send(6, j)
    for k, j in near:
        first_work(k, j)
    for k, j in far:
        first_pass(k, j)
    gather_send(2, 2)
    gather_send(6, 2)
    for k, j in far:
        first_work(k, j)
    def late(k, j):
        dzh, _ = chunk_place(k)
        return (dzh == 1) | (j != 0) | (k == CHUNKS - 1)

    def each_late(k, fn):
        for j in LAST_OWN:
            pl.when(late(k, j))(lambda: fn(column(j)))

    def stage_partial(k):
        each_late(k, lambda b: forward(k, b, 1 - c).wait_recv())
        s = slot(k)
        xs = gath[0, s].reshape(rows, feats)
        ys = gath[1, s].reshape(rows, feats)
        p = [dot_nn(a, w[...]) for a, w in ((xs, wg), (xs, wu), (ys, wd))]

        for b in range(4):
            @pl.when(late(k, b - x))
            def _():
                for n in range(3):
                    q = p[n][b * block:(b + 1) * block]
                    part[k, b, n] = q
                    zsend[k, b, n] = q.astype(BF16)

        @pl.when(is_end)
        def _():
            each_late(k, lambda b: to_pair(k, b).start())

    def stage_forward(k):
        @pl.when(k == 1)
        def _():
            for j in (1, 3, 2):
                gather_x(1, j, column(j)).wait_recv()
                forward(k, column(j), c).start()
            for j in (1, 3, 2):
                gather_send(3, j)
                gather_send(4, j)

        @pl.when(k >= 2)
        def _():
            for j in LAST_OWN:
                @pl.when(late(k, j))
                def _():
                    gather_y(k, j, slot(k), 0).wait_recv()
                    forward(k, column(j), c).start()

        @pl.when(k == 3)
        def _():
            for j in LAST_OWN:
                if j:
                    gather_send(5, j)
                gather_send(7, j)

    def pair_block(k, b):
        to_pair(k, b).wait_recv()
        for n in range(3):
            a = part[k, b, n] + zin1[k, b, n].astype(F32)
            part[k, b, n] = a
            zsend[k, b, n] = a.astype(BF16)
        to_mid(k, b).start()

    def units_block(k, b):
        to_mid(k, b).wait_recv()
        g, u, h = [part[k, b, n] + zin2[k, b, n].astype(F32) for n in range(3)]
        sig = 1.0 / (1.0 + jnp.exp(-g))
        silu = g * sig
        res[k, b, 0] = (silu * u).astype(BF16)
        res[k, b, 1] = (h * u * sig * (1.0 + g * (1.0 - sig))).astype(BF16)
        res[k, b, 2] = (h * silu).astype(BF16)
        to_end(k, b).start()

    def take(*work):
        for fn, (k, j) in work:
            fn(k, column(j))

    first = early

    def stage_mid(i):
        @pl.when(i == 1)
        def _():
            for n in (4, 5):
                take((pair_block, first[n]), (units_block, first[n - 3]))

        @pl.when(i == 2)
        def _():
            for n in (3, 4, 5):
                take((pair_block, (1, LAST_OWN[n - 3])), (units_block, first[n]))
            take((pair_block, (1, LAST_OWN[3])))

        @pl.when(i >= 3)
        def _():
            for j in LAST_OWN:
                @pl.when((i <= CHUNKS) & late(i - 1, j))
                def _():
                    pair_block(i - 1, column(j))

                @pl.when((i <= CHUNKS + 1) & late(i - 2, j))
                def _():
                    units_block(i - 2, column(j))

    def results(k):
        return [res[k, :, n].reshape(rows, units) for n in range(3)]

    def stage_project(k):
        @pl.when(is_end)
        def _():
            for b in range(4):
                to_end(k, b).wait_recv()

        hid, gg, ug = results(k)
        both[k, 0] = dot_nn(hid, wdt[...]).astype(BF16).reshape(both.shape[2:])
        both[k, 1] = (dot_nn(gg, wgt[...]) + dot_nn(ug, wut[...])).astype(BF16).reshape(both.shape[2:])
        to_core(k).start()

    def stage_weights(k):
        hid, gg, ug = results(k)
        s = slot(k)
        xs = gath[0, s].reshape(rows, feats)
        ys = gath[1, s].reshape(rows, feats)
        d_gate[...] += dot_tn(xs, gg)
        d_up[...] += dot_tn(xs, ug)
        d_down[...] += dot_tn(ys, hid)

    def stage_core(k):
        to_core(k).wait_recv()
        xsend[k] = (both[k, c].astype(F32) + cin[k].astype(F32)).astype(BF16)
        for j in (1, 3, 2):
            scatter_x(k, j).start()

    def stage_x(k):
        for j in (1, 3, 2):
            scatter_x(k, j).wait_recv()
        s = xsend[k, x].astype(F32)
        for j in range(3):
            s += xin[k, j].astype(F32)
        ysend[k] = s.astype(BF16)

        @pl.when(k >= 2)
        def _():
            scatter_y(k).start()

    @pl.when(is_mid)
    def _():
        take((pair_block, first[0]))

    half_copy(other).wait_recv()
    forward(1, x, c).start()
    for j in (1, 3, 2):
        gather_x(1, j, x).start()
    for k in (3, 4, 5):
        gather_send(k, 0)

    @pl.when(is_mid)
    def _():
        take((units_block, first[0]))
        for n in (1, 2, 3):
            take((pair_block, first[n]))

    stage_forward(1)

    ahead = 2 * (((zl + 1) // 2) % 2)

    def step(i, _):
        def when(k, fn, cond=None):
            ok = (k >= 0) & (k < CHUNKS)
            pl.when(ok if cond is None else ok & cond)(lambda: fn(k))

        pl.when(is_mid)(lambda: stage_mid(i))
        when(i, stage_partial)
        when(i + 1, stage_forward)
        k = i - 4 + ahead
        when(k - 3, stage_x, k - 3 < CHUNKS - 2)
        when(k - 1, stage_core, k - 1 < CHUNKS - 1)
        when(k, stage_project, k < CHUNKS - 1)
        when(k, stage_weights, k < CHUNKS - 2)
        return 0

    lax.fori_loop(1, CHUNKS + 3, step, 0)
    def total(first, others):
        s = ysend[first].astype(F32)
        for k in others:
            scatter_y(k).wait_recv()
            s += yin[k].astype(F32)
        return s

    end = CHUNKS - 1

    def last_project(j):
        b = column(j)

        @pl.when(is_end)
        def _():
            to_end(end, b).wait_recv()

        hid, gg, ug = res[end, b, 0], res[end, b, 1], res[end, b, 2]
        both[end, 0, b] = dot_nn(hid, wdt[...]).astype(BF16)
        both[end, 1, b] = (dot_nn(gg, wgt[...]) + dot_nn(ug, wut[...])).astype(BF16)
        last_core(b).start()

    def last_scatter(j):
        b = column(j)
        last_core(b).wait_recv()
        xsend[end, b] = (both[end, c, b].astype(F32) + cin[end, b].astype(F32)).astype(BF16)
        if j:
            scatter_x(end, j).start()


    @pl.when(is_end)
    def _():
        stage_core(6)
        stage_x(4)

    last_project(1)
    last_project(3)
    last_scatter(1)
    pl.when(is_end)(lambda: stage_x(5))
    last_project(2)
    last_scatter(3)
    last_project(0)
    last_scatter(2)
    last_scatter(0)
    stage_x(6)
    zhs[...] = total(1, (3, 4, 5)).astype(BF16)
    half_back().start()
    stage_x(end)
    stage_weights(end - 1)
    stage_weights(end)
    s = total(0, (2, 6, 7))
    half_back().wait_recv()
    s += zhin[...].astype(F32)
    fin[...] = (gath[c, own, x].astype(F32) + s).astype(BF16)
    last_copy().start()
    last_copy().wait_recv()
    a, b = fin[...].astype(F32), fin_in[...].astype(F32)
    first = jnp.where(c == 0, a[:half], b[half:])
    second = jnp.where(c == 0, b[:half], a[half:])
    out[...] = first.astype(BF16)
    gtok[...] = second.astype(BF16)

    core_copy().wait_send()
    half_copy(own).wait_send()
    for dzh in (0, 1):
        for j in (1, 2, 3):
            gather_x(dzh, j, x).wait_send()

    def drain(k, _):
        @pl.when(k >= 2)
        def _():
            for j in range(4):
                gather_y(k, j, slot(k), 0).wait_send()
            scatter_y(k).wait_send()

        for b in range(4):
            @pl.when((k != 0) | (b != x))
            def _():
                forward(k, b, c).wait_send()

            @pl.when(is_end)
            def _():
                to_pair(k, b).wait_send()

            @pl.when(is_mid)
            def _():
                to_mid(k, b).wait_send()
                to_end(k, b).wait_send()

        @pl.when(k < CHUNKS - 1)
        def _():
            to_core(k).wait_send()

        for j in (1, 2, 3):
            scatter_x(k, j).wait_send()
        return 0

    lax.fori_loop(0, CHUNKS, drain, 0)
    for b in range(4):
        last_core(b).wait_send()
    half_back().wait_send()
    last_copy().wait_send()


def hand_over(*refs):
    n = (len(refs) - 1) // 2
    sems = refs[-1]
    copies = [pltpu.make_async_copy(refs[i], refs[n + i], sems.at[i]) for i in range(n)]
    for cp in copies:
        cp.start()
    for cp in copies:
        cp.wait()


def on_device(tokens, gate_weight, up_weight, down_weight, grad_out):
    own_rows, feats = tokens.shape
    units = gate_weight.shape[1]
    block = 2 * own_rows
    rows = 4 * block
    dma = pltpu.SemaphoreType.DMA
    vm = pltpu.VMEM
    wshape = (feats, units)
    outs = [(tokens.shape, BF16)] * 2 + [(wshape, F32)] * 3
    any_spec = pl.BlockSpec(memory_space=pl.ANY)
    vmem_spec = pl.BlockSpec(memory_space=pltpu.VMEM)
    made = pl.pallas_call(
        body,
        out_shape=[vm(sh, dt) for sh, dt in outs],
        in_specs=[pl.BlockSpec(memory_space=pltpu.HBM)] * 5,
        out_specs=[vmem_spec] * 5,
        scratch_shapes=[
            vm(tokens.shape, BF16), vm(tokens.shape, BF16),
            vm(wshape, BF16), vm(wshape, BF16), vm(wshape, BF16),
            vm(wshape[::-1], BF16), vm(wshape[::-1], BF16), vm(wshape[::-1], BF16),
            vm((block, feats), BF16), vm((block, feats), BF16),
            vm((2, CHUNKS, 4, block, feats), BF16),
            vm((CHUNKS, 4, 3, block, units), F32),
            vm((CHUNKS, 4, 3, block, units), BF16),
            vm((CHUNKS, 4, 3, block, units), BF16),
            vm((CHUNKS, 4, 3, block, units), BF16),
            vm((CHUNKS, 4, 3, block, units), BF16),
            vm((CHUNKS, 2, 4, block, feats), BF16),
            vm((CHUNKS, 4, block, feats), BF16),
            vm((CHUNKS, 4, block, feats), BF16),
            vm((CHUNKS, 3, block, feats), BF16),
            vm((CHUNKS, block, feats), BF16),
            vm((CHUNKS, block, feats), BF16),
            vm((block, feats), BF16), vm((block, feats), BF16),
            vm((block, feats), BF16), vm((block, feats), BF16),
            dma((5,)),
            dma((2, 1)), dma((2, 1)), dma((2, 2, 3)), dma((2, CHUNKS, 4)), dma((2, CHUNKS, 4)),
            dma((2, CHUNKS, 4)), dma((2, CHUNKS, 4)), dma((2, CHUNKS, 4)), dma((2, CHUNKS)),
            dma((2, 4)), dma((2, CHUNKS, 3)), dma((2, CHUNKS)), dma((2, 1)), dma((2, 1)),
        ],
        compiler_params=pltpu.CompilerParams(
            collective_id=0, has_side_effects=True, vmem_limit_bytes=46 << 20
        ),
        cost_estimate=pl.CostEstimate(
            flops=18 * 8 * rows * feats * units,
            transcendentals=8 * rows * units,
            bytes_accessed=20 * feats * units,
        ),
        name="swiglu_block",
    )(*[
        pltpu.with_memory_space_constraint(a, pltpu.HBM)
        for a in (tokens, grad_out, gate_weight, up_weight, down_weight)
    ])
    return pl.pallas_call(
        hand_over,
        out_shape=[jax.ShapeDtypeStruct(sh, dt) for sh, dt in outs],
        in_specs=[vmem_spec] * len(outs),
        out_specs=[any_spec] * len(outs),
        scratch_shapes=[dma((len(outs),))],
        compiler_params=pltpu.CompilerParams(vmem_limit_bytes=1 << 20),
        name="hand_over",
    )(*made)


def solution(mesh):
    rows_spec = P(("gx", "gy"), "gz")
    weight_spec = P("gz", ("gx", "gy"))
    return jax.shard_map(
        on_device,
        mesh=mesh,
        in_specs=(rows_spec, weight_spec, weight_spec, weight_spec, rows_spec),
        out_specs=(rows_spec, rows_spec, weight_spec, weight_spec, weight_spec),
        check_vma=False,
    )
```

```python
import functools

import jax
import jax.numpy as jnp
from jax import lax
from jax.experimental import pallas as pl
from jax.experimental.pallas import tpu as pltpu
from jax.sharding import PartitionSpec as P

MESH = pl.DeviceIdType.MESH
F32 = jnp.float32
BF16 = jnp.bfloat16
CHUNKS = 8
LAST_OWN = (1, 3, 2, 0)


def chunk_place(k):
    pair, odd = k // 2, k % 2
    late, last = pair // 2, pair // 3
    dzh = (1 - late) * odd + late - last
    dy = late * (3 - odd) + (pair + 2) // 3 - late
    return dzh, dy


def dot_nn(a, b):
    return jnp.dot(a, b, preferred_element_type=F32)


def dot_tn(a, b):
    return lax.dot_general(a, b, (((0,), (0,)), ((), ())), preferred_element_type=F32)


def body(
    tok_any, grd_any, wg_any, wu_any, wd_any,
    out, gtok, d_gate, d_up, d_down,
    tok, grd, wg, wu, wd, wgt, wut, wdt, mine, theirs, gath, part, zsend, zin1, zin2, res,
    both, cin, xsend, xin, ysend, yin, zhs, zhin, fin, fin_in,
    w_sem, cx, zx, xa, ya, fw, z1, z2, z3, co, cl, xr, yr, zr, fo,
):
    gx, gy, zl = lax.axis_index("gx"), lax.axis_index("gy"), lax.axis_index("gz")
    x, zh, y, c = gx // 2, gx % 2, gy // 2, gy % 2
    units = wg.shape[1]
    feats = wg.shape[0]
    block = gath.shape[3]
    rows = 4 * block

    def at(x_, zh_, y_, c_, zl_):
        return (x_ * 2 + zh_, y_ * 2 + c_, zl_)

    def x_peer(j):
        return at((x + j) % 4, zh, y, c, zl)

    def y_peer(j):
        return at(x, zh, (y + j) % 4, c, zl)

    core_peer = at(x, zh, y, 1 - c, zl)
    half_peer = at(x, 1 - zh, y, c, zl)
    pair_z = zl + 1 - 2 * (zl % 2)
    pair_peer = at(x, zh, y, c, pair_z)
    mid_peer = at(x, zh, y, c, 3 - zl)
    is_mid = ((zl + 1) // 2) % 2 == 1
    is_end = ((zl + 1) // 2) % 2 == 0

    def send(src, dst, sems, idx, peer):
        return pltpu.make_async_remote_copy(
            src_ref=src, dst_ref=dst, send_sem=sems.at[(0, *idx)], recv_sem=sems.at[(1, *idx)],
            device_id=peer, device_id_type=MESH,
        )

    def slot(k):
        dzh, dy = chunk_place(k)
        return ((zh + dzh) % 2) * 4 + (y + dy) % 4

    def column(j):
        return (x + j) % 4

    def core_copy():
        return send(mine, theirs, cx, (0,), core_peer)

    def half_copy(place):
        return send(gath.at[c, place, x], gath.at[c, place, x], zx, (0,), half_peer)

    def gather_x(dzh, j, owner):
        place = ((zh + dzh) % 2) * 4 + y
        return send(gath.at[c, place, owner], gath.at[c, place, owner], xa, (dzh, j - 1), x_peer(-j))

    def gather_y(k, j, place, dy):
        b = column(j)
        return send(gath.at[c, place, b], gath.at[c, place, b], ya, (k, j), y_peer(4 - dy))

    def forward(k, b, which):
        s = slot(k)
        return send(gath.at[which, s, b], gath.at[which, s, b], fw, (k, b), core_peer)

    def to_pair(k, b):
        return send(zsend.at[k, b], zin1.at[k, b], z1, (k, b), pair_peer)

    def to_mid(k, b):
        return send(zsend.at[k, b], zin2.at[k, b], z2, (k, b), mid_peer)

    def to_end(k, b):
        return send(res.at[k, b], res.at[k, b], z3, (k, b), pair_peer)

    def to_core(k):
        return send(both.at[k, 1 - c], cin.at[k], co, (k,), core_peer)

    def last_core(b):
        return send(both.at[CHUNKS - 1, 1 - c, b], cin.at[CHUNKS - 1, b], cl, (b,), core_peer)

    def scatter_x(k, j):
        return send(xsend.at[k, (x + j) % 4], xin.at[k, j - 1], xr, (k, j - 1), x_peer(j))

    def scatter_y(k):
        _, dy = chunk_place(k)
        return send(ysend.at[k], yin.at[k], yr, (k,), y_peer(dy))

    def half_back():
        return send(zhs, zhin, zr, (0,), half_peer)

    def last_copy():
        return send(fin, fin_in, fo, (0,), core_peer)

    weight_copies = [
        pltpu.make_async_copy(src, dst, w_sem.at[n])
        for n, (src, dst) in enumerate(((wg_any, wg), (wu_any, wu), (wd_any, wd)))
    ]
    row_copies = [pltpu.make_async_copy(tok_any, tok, w_sem.at[3]), pltpu.make_async_copy(grd_any, grd, w_sem.at[4])]
    for cp in row_copies + weight_copies:
        cp.start()

    peers = [core_peer, half_peer, pair_peer, mid_peer]
    peers += [x_peer(j) for j in (1, 2, 3)] + [y_peer(j) for j in (1, 2, 3)]
    barrier = pltpu.get_barrier_semaphore()
    for peer in peers:
        pl.semaphore_signal(barrier, inc=1, device_id=peer, device_id_type=MESH)
    for cp in row_copies:
        cp.wait()
    mine[...] = jnp.concatenate([tok[...].astype(F32), grd[...].astype(F32)], axis=0).astype(BF16)
    pl.semaphore_wait(barrier, len(peers))

    core_copy().start()
    core_copy().wait_recv()
    m, t = mine[...].astype(F32), theirs[...].astype(F32)
    half = m.shape[0] // 2
    own = zh * 4 + y
    other = (1 - zh) * 4 + y
    for n in range(2):
        mh, th = m[n * half:(n + 1) * half], t[n * half:(n + 1) * half]
        lo = jnp.where(c == 0, mh, th)
        hi = jnp.where(c == 0, th, mh)
        gath[n, own, x] = jnp.concatenate([lo, hi], axis=0).astype(BF16)

    def gather_send(k, j):
        dzh, dy = chunk_place(k)
        gather_y(k, j, ((zh + dzh) % 2) * 4 + y, dy).start()

    half_copy(own).start()
    for j in (1, 3):
        gather_x(0, j, x).start()
    for k in (2, 6):
        gather_send(k, 0)
    gather_x(0, 2, x).start()
    for cp in weight_copies:
        cp.wait()
    for d in (d_gate, d_up, d_down):
        d[...] = jnp.zeros_like(d)

    def block_partial(k, b):
        s = slot(k)
        for n, w in enumerate((wg, wu, wd)):
            p = dot_nn(gath[n // 2, s, b], w[...])
            part[k, b, n] = p
            zsend[k, b, n] = p.astype(BF16)

        @pl.when(is_end)
        def _():
            to_pair(k, b).start()

    def first_pass(k, j):
        if k == 0:
            gather_x(0, j, column(j)).wait_recv()
        else:
            gather_y(k, j, slot(k), 0).wait_recv()
        forward(k, column(j), c).start()

    def first_work(k, j):
        forward(k, column(j), 1 - c).wait_recv()
        block_partial(k, column(j))

    near, far = ((0, 1), (0, 3), (2, 0), (6, 0)), ((0, 2),)
    early = ((0, 0),) + near + far
    block_partial(0, x)
    for flat, turned in ((wg, wgt), (wu, wut), (wd, wdt)):
        turned[...] = flat[...].T
    for k, j in near:
        first_pass(k, j)
    for j in (1, 3):
        gather_send(2, j)
        gather_send(6, j)
    for k, j in near:
        first_work(k, j)
    for k, j in far:
        first_pass(k, j)
    gather_send(2, 2)
    gather_send(6, 2)
    for k, j in far:
        first_work(k, j)
    def late(k, j):
        dzh, _ = chunk_place(k)
        return (dzh == 1) | (j != 0) | (k == CHUNKS - 1)

    def each_late(k, fn):
        for j in LAST_OWN:
            pl.when(late(k, j))(lambda: fn(column(j)))

    def stage_partial(k):
        each_late(k, lambda b: forward(k, b, 1 - c).wait_recv())
        s = slot(k)
        xs = gath[0, s].reshape(rows, feats)
        ys = gath[1, s].reshape(rows, feats)
        p = [dot_nn(a, w[...]) for a, w in ((xs, wg), (xs, wu), (ys, wd))]

        for b in range(4):
            @pl.when(late(k, b - x))
            def _():
                for n in range(3):
                    q = p[n][b * block:(b + 1) * block]
                    part[k, b, n] = q
                    zsend[k, b, n] = q.astype(BF16)

        @pl.when(is_end)
        def _():
            each_late(k, lambda b: to_pair(k, b).start())

    def stage_forward(k):
        @pl.when(k == 1)
        def _():
            for j in (1, 3, 2):
                gather_x(1, j, column(j)).wait_recv()
                forward(k, column(j), c).start()
            for j in (1, 3, 2):
                gather_send(3, j)
                gather_send(4, j)

        @pl.when(k >= 2)
        def _():
            for j in LAST_OWN:
                @pl.when(late(k, j))
                def _():
                    gather_y(k, j, slot(k), 0).wait_recv()
                    forward(k, column(j), c).start()

        @pl.when(k == 3)
        def _():
            for j in LAST_OWN:
                if j:
                    gather_send(5, j)
                gather_send(7, j)

    def pair_block(k, b):
        to_pair(k, b).wait_recv()
        for n in range(3):
            a = part[k, b, n] + zin1[k, b, n].astype(F32)
            part[k, b, n] = a
            zsend[k, b, n] = a.astype(BF16)
        to_mid(k, b).start()

    def units_block(k, b):
        to_mid(k, b).wait_recv()
        g, u, h = [part[k, b, n] + zin2[k, b, n].astype(F32) for n in range(3)]
        sig = 1.0 / (1.0 + jnp.exp(-g))
        silu = g * sig
        res[k, b, 0] = (silu * u).astype(BF16)
        res[k, b, 1] = (h * u * sig * (1.0 + g * (1.0 - sig))).astype(BF16)
        res[k, b, 2] = (h * silu).astype(BF16)
        to_end(k, b).start()

    def take(*work):
        for fn, (k, j) in work:
            fn(k, column(j))

    first = early

    def stage_mid(i):
        @pl.when(i == 1)
        def _():
            for n in (4, 5):
                take((pair_block, first[n]), (units_block, first[n - 3]))

        @pl.when(i == 2)
        def _():
            for n in (3, 4, 5):
                take((pair_block, (1, LAST_OWN[n - 3])), (units_block, first[n]))
            take((pair_block, (1, LAST_OWN[3])))

        @pl.when(i >= 3)
        def _():
            for j in LAST_OWN:
                @pl.when((i <= CHUNKS) & late(i - 1, j))
                def _():
                    pair_block(i - 1, column(j))

                @pl.when((i <= CHUNKS + 1) & late(i - 2, j))
                def _():
                    units_block(i - 2, column(j))

    def results(k):
        return [res[k, :, n].reshape(rows, units) for n in range(3)]

    def stage_project(k):
        @pl.when(is_end)
        def _():
            for b in range(4):
                to_end(k, b).wait_recv()

        hid, gg, ug = results(k)
        both[k, 0] = dot_nn(hid, wdt[...]).astype(BF16).reshape(both.shape[2:])
        both[k, 1] = (dot_nn(gg, wgt[...]) + dot_nn(ug, wut[...])).astype(BF16).reshape(both.shape[2:])
        to_core(k).start()

    def stage_weights(k):
        hid, gg, ug = results(k)
        s = slot(k)
        xs = gath[0, s].reshape(rows, feats)
        ys = gath[1, s].reshape(rows, feats)
        d_gate[...] += dot_tn(xs, gg)
        d_up[...] += dot_tn(xs, ug)
        d_down[...] += dot_tn(ys, hid)

    def stage_core(k):
        to_core(k).wait_recv()
        xsend[k] = (both[k, c].astype(F32) + cin[k].astype(F32)).astype(BF16)
        for j in (1, 3, 2):
            scatter_x(k, j).start()

    def stage_x(k):
        for j in (1, 3, 2):
            scatter_x(k, j).wait_recv()
        s = xsend[k, x].astype(F32)
        for j in range(3):
            s += xin[k, j].astype(F32)
        ysend[k] = s.astype(BF16)

        @pl.when(k >= 2)
        def _():
            scatter_y(k).start()

    @pl.when(is_mid)
    def _():
        take((pair_block, first[0]))

    half_copy(other).wait_recv()
    forward(1, x, c).start()
    for j in (1, 3, 2):
        gather_x(1, j, x).start()
    for k in (3, 4, 5):
        gather_send(k, 0)

    @pl.when(is_mid)
    def _():
        take((units_block, first[0]))
        for n in (1, 2, 3):
            take((pair_block, first[n]))

    stage_forward(1)

    ahead = 2 * (((zl + 1) // 2) % 2)

    def step(i, _):
        def when(k, fn, cond=None):
            ok = (k >= 0) & (k < CHUNKS)
            pl.when(ok if cond is None else ok & cond)(lambda: fn(k))

        pl.when(is_mid)(lambda: stage_mid(i))
        when(i, stage_partial)
        when(i + 1, stage_forward)
        k = i - 4 + ahead
        when(k - 3, stage_x, k - 3 < CHUNKS - 3)
        when(k - 1, stage_core, k - 1 < CHUNKS - 1)
        when(k, stage_project, k < CHUNKS - 1)
        when(k - 1, stage_weights, k - 1 < CHUNKS - 4)
        return 0

    lax.fori_loop(1, CHUNKS + 3, step, 0)
    def total(first, others):
        s = ysend[first].astype(F32)
        for k in others:
            scatter_y(k).wait_recv()
            s += yin[k].astype(F32)
        return s

    end = CHUNKS - 1

    def last_project(j):
        b = column(j)

        @pl.when(is_end)
        def _():
            to_end(end, b).wait_recv()

        hid, gg, ug = res[end, b, 0], res[end, b, 1], res[end, b, 2]
        both[end, 0, b] = dot_nn(hid, wdt[...]).astype(BF16)
        both[end, 1, b] = (dot_nn(gg, wgt[...]) + dot_nn(ug, wut[...])).astype(BF16)
        last_core(b).start()

    def last_scatter(j):
        b = column(j)
        last_core(b).wait_recv()
        xsend[end, b] = (both[end, c, b].astype(F32) + cin[end, b].astype(F32)).astype(BF16)
        if j:
            scatter_x(end, j).start()


    @pl.when(is_end)
    def _():
        stage_core(6)
        stage_x(4)

    last_project(1)
    last_project(3)
    last_scatter(1)
    stage_x(5)
    last_project(2)
    last_scatter(3)
    last_project(0)
    last_scatter(2)
    last_scatter(0)
    stage_x(6)
    zhs[...] = total(1, (3, 4, 5)).astype(BF16)
    half_back().start()
    stage_x(end)
    for k in range(CHUNKS - 4, CHUNKS):
        stage_weights(k)
    s = total(0, (2, 6, 7))
    half_back().wait_recv()
    s += zhin[...].astype(F32)
    fin[...] = (gath[c, own, x].astype(F32) + s).astype(BF16)
    last_copy().start()
    last_copy().wait_recv()
    a, b = fin[...].astype(F32), fin_in[...].astype(F32)
    first = jnp.where(c == 0, a[:half], b[half:])
    second = jnp.where(c == 0, b[:half], a[half:])
    out[...] = first.astype(BF16)
    gtok[...] = second.astype(BF16)

    core_copy().wait_send()
    half_copy(own).wait_send()
    for dzh in (0, 1):
        for j in (1, 2, 3):
            gather_x(dzh, j, x).wait_send()

    def drain(k, _):
        @pl.when(k >= 2)
        def _():
            for j in range(4):
                gather_y(k, j, slot(k), 0).wait_send()
            scatter_y(k).wait_send()

        for b in range(4):
            @pl.when((k != 0) | (b != x))
            def _():
                forward(k, b, c).wait_send()

            @pl.when(is_end)
            def _():
                to_pair(k, b).wait_send()

            @pl.when(is_mid)
            def _():
                to_mid(k, b).wait_send()
                to_end(k, b).wait_send()

        @pl.when(k < CHUNKS - 1)
        def _():
            to_core(k).wait_send()

        for j in (1, 2, 3):
            scatter_x(k, j).wait_send()
        return 0

    lax.fori_loop(0, CHUNKS, drain, 0)
    for b in range(4):
        last_core(b).wait_send()
    half_back().wait_send()
    last_copy().wait_send()


def hand_over(*refs):
    n = (len(refs) - 1) // 2
    sems = refs[-1]
    copies = [pltpu.make_async_copy(refs[i], refs[n + i], sems.at[i]) for i in range(n)]
    for cp in copies:
        cp.start()
    for cp in copies:
        cp.wait()


def on_device(tokens, gate_weight, up_weight, down_weight, grad_out):
    own_rows, feats = tokens.shape
    units = gate_weight.shape[1]
    block = 2 * own_rows
    rows = 4 * block
    dma = pltpu.SemaphoreType.DMA
    vm = pltpu.VMEM
    wshape = (feats, units)
    outs = [(tokens.shape, BF16)] * 2 + [(wshape, F32)] * 3
    any_spec = pl.BlockSpec(memory_space=pl.ANY)
    vmem_spec = pl.BlockSpec(memory_space=pltpu.VMEM)
    made = pl.pallas_call(
        body,
        out_shape=[vm(sh, dt) for sh, dt in outs],
        in_specs=[pl.BlockSpec(memory_space=pltpu.HBM)] * 5,
        out_specs=[vmem_spec] * 5,
        scratch_shapes=[
            vm(tokens.shape, BF16), vm(tokens.shape, BF16),
            vm(wshape, BF16), vm(wshape, BF16), vm(wshape, BF16),
            vm(wshape[::-1], BF16), vm(wshape[::-1], BF16), vm(wshape[::-1], BF16),
            vm((block, feats), BF16), vm((block, feats), BF16),
            vm((2, CHUNKS, 4, block, feats), BF16),
            vm((CHUNKS, 4, 3, block, units), F32),
            vm((CHUNKS, 4, 3, block, units), BF16),
            vm((CHUNKS, 4, 3, block, units), BF16),
            vm((CHUNKS, 4, 3, block, units), BF16),
            vm((CHUNKS, 4, 3, block, units), BF16),
            vm((CHUNKS, 2, 4, block, feats), BF16),
            vm((CHUNKS, 4, block, feats), BF16),
            vm((CHUNKS, 4, block, feats), BF16),
            vm((CHUNKS, 3, block, feats), BF16),
            vm((CHUNKS, block, feats), BF16),
            vm((CHUNKS, block, feats), BF16),
            vm((block, feats), BF16), vm((block, feats), BF16),
            vm((block, feats), BF16), vm((block, feats), BF16),
            dma((5,)),
            dma((2, 1)), dma((2, 1)), dma((2, 2, 3)), dma((2, CHUNKS, 4)), dma((2, CHUNKS, 4)),
            dma((2, CHUNKS, 4)), dma((2, CHUNKS, 4)), dma((2, CHUNKS, 4)), dma((2, CHUNKS)),
            dma((2, 4)), dma((2, CHUNKS, 3)), dma((2, CHUNKS)), dma((2, 1)), dma((2, 1)),
        ],
        compiler_params=pltpu.CompilerParams(
            collective_id=0, has_side_effects=True, vmem_limit_bytes=46 << 20
        ),
        cost_estimate=pl.CostEstimate(
            flops=18 * 8 * rows * feats * units,
            transcendentals=8 * rows * units,
            bytes_accessed=20 * feats * units,
        ),
        name="swiglu_block",
    )(*[
        pltpu.with_memory_space_constraint(a, pltpu.HBM)
        for a in (tokens, grad_out, gate_weight, up_weight, down_weight)
    ])
    return pl.pallas_call(
        hand_over,
        out_shape=[jax.ShapeDtypeStruct(sh, dt) for sh, dt in outs],
        in_specs=[vmem_spec] * len(outs),
        out_specs=[any_spec] * len(outs),
        scratch_shapes=[dma((len(outs),))],
        compiler_params=pltpu.CompilerParams(vmem_limit_bytes=1 << 20),
        name="hand_over",
    )(*made)


def solution(mesh):
    rows_spec = P(("gx", "gy"), "gz")
    weight_spec = P("gz", ("gx", "gy"))
    return jax.shard_map(
        on_device,
        mesh=mesh,
        in_specs=(rows_spec, weight_spec, weight_spec, weight_spec, rows_spec),
        out_specs=(rows_spec, rows_spec, weight_spec, weight_spec, weight_spec),
        check_vma=False,
    )
```
